32 devices in a mesh: parts: 2 (over y), dp: 4 (over z), tp: 4 (over x, core).
Axes of the slice: x: 2, y: 2, z: 4, core: 2. Of those that a mesh axis runs over, the one named last changes fastest.
Arguments:
- kcache: bfloat16 [768, 64, 1024], P(('parts', 'dp'), None, 'tp'), parts along dimension 0, may hold values from -6 to 6
- vcache: bfloat16 [768, 64, 1024], P(('parts', 'dp'), None, 'tp'), parts along dimension 0, may hold values from -6 to 6
- send_pages: int32 [8, 4, 3], P(('parts', 'dp')), parts along dimension 0, may hold values from -1 to 95, as said below
- tables: int32 [32, 16], P(('parts', 'dp')), parts along dimension 0, may hold values from 0 to 107, as said below
- lengths: int32 [32], P(('parts', 'dp')), parts along dimension 0, may hold values from 1 to 1020, as said below
- queries: bfloat16 [32, 4, 8192], P(('parts', 'dp'), None, 'tp'), parts along dimension 0, may hold values from -120 to 120
- new_keys: bfloat16 [32, 4, 1024], P(('parts', 'dp'), None, 'tp'), parts along dimension 0, may hold values from -6 to 6
- new_values: bfloat16 [32, 4, 1024], P(('parts', 'dp'), None, 'tp'), parts along dimension 0, may hold values from -6 to 6
- pre_mix: float32 [64, 64], replicated, may hold values from -1.5 to 1.5
- post_mix: float32 [64, 64], replicated, may hold values from -1.5 to 1.5
Outputs:
- attended: bfloat16 [32, 4, 8192], P(('parts', 'dp'), None, 'tp'), parts along dimension 0
The draws below stay inside these ranges and needn't reach their ends.
There are 2 independent parts, one for each index of `parts`. The reference program is written for one: setup_inputs(seed, part) draws one part's arguments, and reference() takes and returns one part's arrays. A program takes and returns all parts, laid end to end along the dimension named above; an argument that names none is the same for every part. Nothing has to cross between parts.
Inputs may be any that keep to these rules, and one draw needn't show every extreme that they name: `send_pages`: each entry is a page id of the source replica or -1; no replica sends to itself; in every draw some source fills all 3 slots to every other replica and some target receives 3 pages from every other source. `tables`: entries name a replica's own pages (below 96) or extended slots 96 + s * 3 + c whose send_pages[s, r, c] is not -1; a page may be named more than once. `lengths`: some sequence has exactly 1020 cached tokens in every draw.
All inputs are finite; a program needn't handle non-finite values.
Results may differ from the reference program's by a relative error of at most 0.0051.
Values may be sent and summed in bfloat16 or wider, within the bound.
A program may use at most 128 MiB of HBM per device.

```python
import jax
import jax.numpy as jnp
from jax import lax

HEADS = 64
KV_HEADS = 8
HEAD = 128
STEPS = 4
PAGE = 64
CAP = 3
SLOTS = 4
MAXP = 16
PAGES = 96
MAXLEN = 1024
ROWS = 16
POOL = 384
N_DP = 4


def page_moves(key):
    moved_key = jax.random.fold_in(key, 101)
    first_key, second_key, third_key = jax.random.split(moved_key, 3)
    page_ids = jax.random.randint(first_key, (N_DP, N_DP, CAP), 0, PAGES)
    filled = jax.random.randint(second_key, (N_DP, N_DP, CAP), 0, 5) < 3
    source = jnp.arange(N_DP, dtype=jnp.int32)[:, None, None]
    target = jnp.arange(N_DP, dtype=jnp.int32)[None, :, None]
    chosen = jax.random.randint(third_key, (2,), 0, N_DP)
    filled = filled | (target == chosen[1]) | (source == chosen[0])
    filled = filled & (source != target)
    return jnp.where(filled, page_ids, -1).astype(jnp.int32)


def shared_keys(key):
    second_key = jax.random.fold_in(jax.random.fold_in(key, 202), 1)
    own_part = jax.random.normal(second_key, (ROWS, STEPS, KV_HEADS * HEAD), jnp.float32)
    return jnp.clip(own_part, -6.0, 6.0)


def draw_send_pages(key, part):
    return page_moves(key)


def draw_tables(key, part):
    moves = page_moves(key)
    key = jax.random.fold_in(key, 7)
    first_key, second_key = jax.random.split(key)
    extent = PAGES + N_DP * CAP
    arriving = jnp.transpose(moves >= 0, (1, 0, 2)).reshape(N_DP, N_DP * CAP)
    usable = jnp.concatenate([jnp.ones((N_DP, PAGES), bool), arriving], 1)
    ranking = jax.random.randint(first_key, (N_DP, extent), 0, extent) * extent + jnp.arange(extent, dtype=jnp.int32)[None, :]
    ranking = ranking + jnp.where(usable, 0, extent * extent)
    ordering = jnp.argsort(ranking, axis=1, stable=True)
    usable_count = jnp.sum(usable.astype(jnp.int32), axis=1)
    picked = jax.random.randint(second_key, (N_DP, SLOTS * MAXP), 0, usable_count[:, None])
    table_ids = jnp.take_along_axis(ordering, picked, axis=1)
    return table_ids.reshape(ROWS, MAXP).astype(jnp.int32)


def draw_lengths(key, part):
    key = jax.random.fold_in(key, 11)
    first_key, second_key, third_key = jax.random.split(key, 3)
    longest = MAXLEN - STEPS
    first_draw = jax.random.randint(first_key, (ROWS,), 0, longest)
    second_draw = jax.random.randint(second_key, (ROWS,), 0, longest)
    row_lengths = 1 + first_draw * second_draw // longest
    chosen = jax.random.randint(third_key, (), 0, ROWS)
    return jnp.where(jnp.arange(ROWS) == chosen, longest, row_lengths).astype(jnp.int32)


def draw_new_keys(key, part):
    key_rows = shared_keys(key)
    return key_rows.astype(jnp.bfloat16)


def draw_queries(key, part):
    key = jax.random.fold_in(key, 5)
    drawn_rows = jnp.clip(jax.random.normal(key, (ROWS, STEPS, HEADS * HEAD), jnp.float32), -6.0, 6.0)
    return drawn_rows.astype(jnp.bfloat16)


def mixing_matrix(key):
    first_key, second_key = jax.random.split(key)
    diagonal = jax.random.uniform(first_key, (HEADS,), jnp.float32, 0.7, 1.3)
    off_diagonal = jnp.clip(0.05 * jax.random.normal(second_key, (HEADS, HEADS), jnp.float32), -0.3, 0.3)
    identity = jnp.eye(HEADS, dtype=jnp.float32)
    return identity * diagonal[None, :] + (1.0 - identity) * off_diagonal


def draw_pre_mix(key, part):
    key = jax.random.fold_in(key, 21)
    return mixing_matrix(key)


def draw_post_mix(key, part):
    key = jax.random.fold_in(key, 22)
    return mixing_matrix(key)


def level_of(stream_key, dims, shards, least, top_value):
    level, own = 1.0, jax.random.fold_in(stream_key, 6)
    for dim, blocks in shards:
        steps = jnp.exp(jax.random.uniform(jax.random.fold_in(own, dim), (blocks,), jnp.float32, least / len(shards), top_value / len(shards)))
        level = level * jnp.repeat(steps, dims[dim] // blocks).reshape([-1 if axis == dim else 1 for axis in range(len(dims))])
    return level


def centred(stream_key, dims, scale, limit, shards=(), kind=jnp.bfloat16):
    level = level_of(stream_key, dims, shards, -0.22, 0.18) if shards else 1.0
    entries = jax.random.normal(stream_key, dims, jnp.float32) * scale * level
    return jnp.minimum(jnp.maximum(entries, -limit), limit).astype(kind)


def setup_inputs(seed: int = 0, part: int = 0) -> dict:
    seeds = jax.random.split(jax.random.key(seed), 11)
    own_keys = jax.random.split(jax.random.fold_in(seeds[10], part), 11)
    kcache = centred(own_keys[0], (POOL, PAGE, KV_HEADS * HEAD), 1.0, 6.0, ((0, 4), (2, 4)))
    vcache = centred(own_keys[1], (POOL, PAGE, KV_HEADS * HEAD), 1.0, 6.0, ((0, 4), (2, 4)))
    send_pages = draw_send_pages(jax.random.fold_in(jax.random.fold_in(seeds[10], part), 71), part)
    tables = draw_tables(jax.random.fold_in(jax.random.fold_in(seeds[10], part), 71), part)
    lengths = draw_lengths(jax.random.fold_in(jax.random.fold_in(seeds[10], part), 71), part)
    queries = draw_queries(jax.random.fold_in(jax.random.fold_in(seeds[10], part), 71), part)
    new_keys = draw_new_keys(jax.random.fold_in(jax.random.fold_in(seeds[10], part), 71), part)
    new_values = centred(own_keys[7], (ROWS, STEPS, KV_HEADS * HEAD), 1.0, 6.0, ((0, 4), (2, 4)))
    pre_mix = draw_pre_mix(jax.random.fold_in(seeds[10], 71), part)
    post_mix = draw_post_mix(jax.random.fold_in(seeds[10], 71), part)
    return {"kcache": kcache, "vcache": vcache, "send_pages": send_pages, "tables": tables, "lengths": lengths, "queries": queries, "new_keys": new_keys, "new_values": new_values, "pre_mix": pre_mix, "post_mix": post_mix}


def softmax_rows(scores, visible):
    masked = jnp.where(visible, scores, -jnp.inf)
    row_max = jnp.max(masked, axis=-1, keepdims=True)
    raised = jnp.exp(masked - row_max)
    return raised / jnp.sum(raised, axis=-1, keepdims=True)


def attention(query_rows, key_rows, value_rows, row_lengths, pre_mix, post_mix):
    group_size = HEADS // KV_HEADS
    highest = lax.Precision.HIGHEST
    query_blocks = query_rows.astype(jnp.float32).reshape(SLOTS, STEPS, KV_HEADS, group_size, HEAD)
    key_blocks = key_rows.astype(jnp.float32).reshape(SLOTS, MAXLEN, KV_HEADS, HEAD)
    value_blocks = value_rows.astype(jnp.float32).reshape(SLOTS, MAXLEN, KV_HEADS, HEAD)
    logits = jnp.einsum('stgrd,sjgd->stgrj', query_blocks, key_blocks, precision=highest) * (HEAD ** -0.5)
    logits = logits.reshape(SLOTS, STEPS, HEADS, MAXLEN)
    mixed_scores = jnp.einsum('hk,sthj->stkj', pre_mix, logits, precision=highest)
    position = jnp.arange(MAXLEN, dtype=jnp.int32)
    visible = position[None, None, :] <= row_lengths[:, None, None] + jnp.arange(STEPS, dtype=jnp.int32)[None, :, None]
    weights = softmax_rows(mixed_scores, visible[:, :, None, :])
    blended = jnp.einsum('hk,sthj->stkj', post_mix, weights, precision=highest).astype(jnp.bfloat16)
    blended = blended.astype(jnp.float32).reshape(SLOTS, STEPS, KV_HEADS, group_size, MAXLEN)
    outputs = jnp.einsum('stgrj,sjgd->stgrd', blended, value_blocks, precision=highest)
    return outputs.reshape(SLOTS, STEPS, HEADS * HEAD).astype(jnp.bfloat16)


def insert_new(cache_rows, fresh_rows, offset):
    return lax.dynamic_update_slice(cache_rows, fresh_rows, (offset, jnp.zeros((), jnp.int32)))


def reference(kcache, vcache, send_pages, tables, lengths, queries, new_keys, new_values, pre_mix, post_mix):
    width_all = KV_HEADS * HEAD
    pool_keys = kcache.reshape(N_DP, PAGES, PAGE, width_all)
    pool_values = vcache.reshape(N_DP, PAGES, PAGE, width_all)
    sources = jnp.arange(N_DP, dtype=jnp.int32)

    def incoming(pool, target):
        page_ids = send_pages[:, target, :]
        present = page_ids >= 0
        safe_ids = jnp.where(present, page_ids, 0)
        fetched = pool[sources[:, None], safe_ids]
        fetched = jnp.where(present[:, :, None, None], fetched, jnp.zeros((), pool.dtype))
        return fetched.reshape(N_DP * CAP, PAGE, width_all)

    def replica(target):
        extended_keys = jnp.concatenate([pool_keys[target], incoming(pool_keys, target)], 0)
        extended_values = jnp.concatenate([pool_values[target], incoming(pool_values, target)], 0)
        first_row = target * SLOTS
        table_rows = lax.dynamic_slice_in_dim(tables, first_row, SLOTS, 0)
        row_lengths = lax.dynamic_slice_in_dim(lengths, first_row, SLOTS, 0)
        key_rows = extended_keys[table_rows].reshape(SLOTS, MAXLEN, width_all)
        value_rows = extended_values[table_rows].reshape(SLOTS, MAXLEN, width_all)
        key_rows = jax.vmap(insert_new)(key_rows, lax.dynamic_slice_in_dim(new_keys, first_row, SLOTS, 0), row_lengths)
        value_rows = jax.vmap(insert_new)(value_rows, lax.dynamic_slice_in_dim(new_values, first_row, SLOTS, 0), row_lengths)
        query_rows = lax.dynamic_slice_in_dim(queries, first_row, SLOTS, 0)
        return attention(query_rows, key_rows, value_rows, row_lengths, pre_mix, post_mix)

    results = lax.map(replica, sources)
    return results.reshape(ROWS, STEPS, HEADS * HEAD)
```

```python
import functools

import jax
import jax.numpy as jnp
from jax import lax
from jax.experimental import pallas as pl
from jax.experimental.pallas import tpu as pltpu
from jax.sharding import PartitionSpec as P

HEAD = 128
MESH = pl.DeviceIdType.MESH
HIGHEST = lax.Precision.HIGHEST


def each(count, body):
    if count <= 4:
        for step in range(count):
            body(step)
    else:

        def looped(step, carry):
            body(step)
            return carry

        lax.fori_loop(0, count, looped, 0)


def kernel(
    n_dp,
    n_tp,
    send_ref,
    tables_ref,
    lengths_ref,
    kcache_ref,
    vcache_ref,
    queries_ref,
    newk_ref,
    newv_ref,
    pre_ref,
    post_ref,
    out_ref,
    ext_k,
    ext_v,
    stage_k,
    stage_v,
    in_k,
    in_v,
    q_wide,
    key_rows,
    value_rows,
    raw_send,
    raw_all,
    mix_t,
    blend_send,
    blend_in,
    res,
    load_sem,
    ks_sem,
    kr_sem,
    vs_sem,
    vr_sem,
    rs_sem,
    rr_sem,
    bs_sem,
    br_sem,
):
    pages, page_len, width = kcache_ref.shape
    cap = send_ref.shape[2]
    slots, maxp = tables_ref.shape
    steps = queries_ref.shape[1]
    heads = queries_ref.shape[2] // HEAD
    groups = width // HEAD
    group_size = heads // groups
    span = maxp * page_len
    dp = lax.axis_index("dp")
    tp = lax.axis_index("tp")

    barrier = pltpu.get_barrier_semaphore()
    for o in range(1, n_dp):
        pl.semaphore_signal(
            barrier, inc=1, device_id={"dp": lax.rem(dp + o, n_dp)}, device_id_type=MESH
        )
    for o in range(1, n_tp):
        pl.semaphore_signal(
            barrier, inc=1, device_id={"tp": lax.rem(tp + o, n_tp)}, device_id_type=MESH
        )

    parts = load_sem.shape[1]
    chunk = pages // parts

    def load(which, cache, ext, part):
        rows = pl.ds(part * chunk, chunk)
        return pltpu.make_async_copy(cache.at[rows], ext.at[rows], load_sem.at[which, part])

    for part in range(parts):
        load(0, kcache_ref, ext_k, part).start()
    for part in range(parts):
        load(1, vcache_ref, ext_v, part).start()

    def page_copy(stage, inbox, s_sem, r_sem, o):
        return pltpu.make_async_remote_copy(
            src_ref=stage.at[pl.ds(o * cap, cap)],
            dst_ref=inbox.at[pl.ds(dp * cap, cap)],
            send_sem=s_sem.at[o],
            recv_sem=r_sem.at[o],
            device_id={"dp": lax.rem(dp + o + 1, n_dp)},
            device_id_type=MESH,
        )

    def stage_pages(stage, ext, o):
        target = lax.rem(dp + o + 1, n_dp)
        for c in range(cap):
            page = jnp.maximum(send_ref[0, target, c], 0)
            stage[o * cap + c] = ext[page]

    pl.semaphore_wait(barrier, n_dp + n_tp - 2)
    for part in range(parts):
        load(0, kcache_ref, ext_k, part).wait()

    def send_k(o):
        stage_pages(stage_k, ext_k, o)
        page_copy(stage_k, in_k, ks_sem, kr_sem, o).start()

    each(n_dp - 1, send_k)

    q_wide[...] = jnp.zeros_like(q_wide)
    for s in range(slots):
        for h in range(heads):
            g = h // group_size
            q_wide[s, g, pl.ds(h, steps, stride=heads), :] = queries_ref[
                s, :, h * HEAD : (h + 1) * HEAD
            ].astype(jnp.float32)
    mix_t[0] = pre_ref[...].T
    mix_t[1] = post_ref[...].T

    for part in range(parts):
        load(1, vcache_ref, ext_v, part).wait()
    each(n_dp - 1, lambda o: stage_pages(stage_v, ext_v, o))

    def take_in(inbox, ext, copy):
        def body(o):
            copy(o).wait_recv()
            source = lax.rem(dp + n_dp - 1 - o, n_dp)
            for c in range(cap):
                ext[pages + source * cap + c] = inbox[source * cap + c]

        each(n_dp - 1, body)

    take_in(in_k, ext_k, lambda o: page_copy(stage_k, in_k, ks_sem, kr_sem, o))
    each(n_dp - 1, lambda o: page_copy(stage_v, in_v, vs_sem, vr_sem, o).start())

    position = lax.broadcasted_iota(jnp.int32, (steps * heads, span), 1)

    def raw_of(s):
        for p in range(maxp):
            key_rows[pl.ds(p * page_len, page_len), :] = ext_k[tables_ref[s, p]]
        rows = jnp.concatenate([q_wide[s, g] for g in range(groups)], axis=1).astype(
            jnp.bfloat16
        )
        contract = (((1,), (1,)), ((), ()))
        raw = lax.dot_general(
            rows, key_rows[...], contract, preferred_element_type=jnp.float32
        )
        fresh = lax.dot_general(
            rows, newk_ref[s], contract, preferred_element_type=jnp.float32
        )
        first = lengths_ref[s]
        for t in range(steps):
            raw = jnp.where(position == first + t, fresh[:, t : t + 1], raw)
        return raw * (HEAD ** (-0.5))

    def raw_copy(o, t):
        return pltpu.make_async_remote_copy(
            src_ref=raw_send.at[o - 1, t],
            dst_ref=raw_all.at[t, pl.ds(tp * heads, heads)],
            send_sem=rs_sem.at[o - 1, t],
            recv_sem=rr_sem.at[o - 1, t],
            device_id={"tp": lax.rem(tp + o, n_tp)},
            device_id_type=MESH,
        )

    half = n_tp // 2
    order = [half] + [o for o in range(1, n_tp) if o != half]
    early = steps // 2
    for o in order:
        raw = raw_of(lax.rem(tp + o, n_tp))
        for t in range(steps):
            raw_send[o - 1, t] = raw[t * heads : (t + 1) * heads]
        for t in range(early):
            raw_copy(o, t).start()
    for t in range(early, steps):
        for o in order:
            raw_copy(o, t).start()
    raw = raw_of(tp)
    for t in range(steps):
        raw_all[t, pl.ds(tp * heads, heads), :] = raw[t * heads : (t + 1) * heads]

    def blend_copy(o, t):
        peer = lax.rem(tp + o, n_tp)
        return pltpu.make_async_remote_copy(
            src_ref=blend_send.at[t, pl.ds(peer * heads, heads)],
            dst_ref=blend_in.at[tp, pl.ds(t * heads, heads)],
            send_sem=bs_sem.at[o - 1, t],
            recv_sem=br_sem.at[o - 1, t],
            device_id={"tp": peer},
            device_id_type=MESH,
        )

    spot = lax.broadcasted_iota(jnp.int32, (n_tp * heads, span), 1)
    own_length = lengths_ref[tp]

    def mix(t):
        for o in order:
            raw_copy(o, t).wait_recv()
        mixed = jnp.dot(
            mix_t[0], raw_all[t], precision=HIGHEST, preferred_element_type=jnp.float32
        )
        mixed = jnp.where(spot <= own_length + t, mixed, -jnp.inf)
        raised = jnp.exp(mixed - jnp.max(mixed, axis=1, keepdims=True))
        weights = raised / jnp.sum(raised, axis=1, keepdims=True)
        blended = jnp.dot(
            mix_t[1], weights, precision=HIGHEST, preferred_element_type=jnp.float32
        )
        blend_send[t] = blended.astype(jnp.bfloat16)
        for o in order:
            blend_copy(o, t).start()
        blend_in[tp, pl.ds(t * heads, heads), :] = blend_send[t, pl.ds(tp * heads, heads), :]

    row = lax.broadcasted_iota(jnp.int32, (page_len, width), 0)

    def gather_values(s):
        first = lengths_ref[s]
        fresh = newv_ref[s].astype(jnp.float32)
        for p in range(maxp):
            page = ext_v[tables_ref[s, p]].astype(jnp.float32)
            for t in range(steps):
                page = jnp.where(row == first + t - p * page_len, fresh[t : t + 1, :], page)
            value_rows[s, pl.ds(p * page_len, page_len), :] = page.astype(jnp.bfloat16)

    for t in range(steps - 1):
        mix(t)
    take_in(in_v, ext_v, lambda o: page_copy(stage_v, in_v, vs_sem, vr_sem, o))
    for s in range(slots):
        gather_values(s)
    mix(steps - 1)

    for o in [0] + [n_tp - o for o in order]:
        s = lax.rem(tp + o, n_tp)
        if o:
            for t in range(steps):
                blend_copy(n_tp - o, t).wait_recv()
        result = jnp.dot(blend_in[s], value_rows[s], preferred_element_type=jnp.float32)
        for g in range(groups):
            res[g] = result[:, g * HEAD : (g + 1) * HEAD]
        for h in range(heads):
            out_ref[s, :, h * HEAD : (h + 1) * HEAD] = res[
                h // group_size, pl.ds(h, steps, stride=heads), :
            ].astype(out_ref.dtype)

    def all_sent(o):
        page_copy(stage_k, in_k, ks_sem, kr_sem, o).wait_send()
        page_copy(stage_v, in_v, vs_sem, vr_sem, o).wait_send()

    each(n_dp - 1, all_sent)
    for t in range(steps):
        for o in order:
            raw_copy(o, t).wait_send()
            blend_copy(o, t).wait_send()


def on_device(
    n_dp,
    n_tp,
    kcache,
    vcache,
    send_pages,
    tables,
    lengths,
    queries,
    new_keys,
    new_values,
    pre_mix,
    post_mix,
):
    pages, page_len, width = kcache.shape
    cap = send_pages.shape[2]
    slots, maxp = tables.shape
    steps = queries.shape[1]
    heads = queries.shape[2] // HEAD
    groups = width // HEAD
    span = maxp * page_len
    all_heads = heads * n_tp
    load_parts = 4
    vmem = pl.BlockSpec(memory_space=pltpu.VMEM)
    smem = pl.BlockSpec(memory_space=pltpu.SMEM)
    hbm = pl.BlockSpec(memory_space=pl.ANY)
    moved = (n_dp - 1) * cap
    bf16, f32 = jnp.bfloat16, jnp.float32
    dma = pltpu.SemaphoreType.DMA
    return pl.pallas_call(
        functools.partial(kernel, n_dp, n_tp),
        out_shape=jax.ShapeDtypeStruct(queries.shape, bf16),
        in_specs=[smem, smem, smem, hbm, hbm, vmem, vmem, vmem, vmem, vmem],
        out_specs=vmem,
        scratch_shapes=[
            pltpu.VMEM((pages + n_dp * cap, page_len, width), bf16),
            pltpu.VMEM((pages + n_dp * cap, page_len, width), bf16),
            pltpu.VMEM((moved, page_len, width), bf16),
            pltpu.VMEM((moved, page_len, width), bf16),
            pltpu.VMEM((n_dp * cap, page_len, width), bf16),
            pltpu.VMEM((n_dp * cap, page_len, width), bf16),
            pltpu.VMEM((slots, groups, steps * heads, HEAD), f32),
            pltpu.VMEM((span, width), bf16),
            pltpu.VMEM((slots, span, width), bf16),
            pltpu.VMEM((n_tp - 1, steps, heads, span), f32),
            pltpu.VMEM((steps, all_heads, span), f32),
            pltpu.VMEM((2, all_heads, all_heads), f32),
            pltpu.VMEM((steps, all_heads, span), bf16),
            pltpu.VMEM((slots, steps * heads, span), bf16),
            pltpu.VMEM((groups, steps * heads, HEAD), f32),
            dma((2, load_parts)),
            dma((n_dp - 1,)),
            dma((n_dp - 1,)),
            dma((n_dp - 1,)),
            dma((n_dp - 1,)),
            dma((n_tp - 1, steps)),
            dma((n_tp - 1, steps)),
            dma((n_tp - 1, steps)),
            dma((n_tp - 1, steps)),
        ],
        compiler_params=pltpu.CompilerParams(
            collective_id=0, has_side_effects=True, vmem_limit_bytes=48 * 1024 * 1024
        ),
    )(
        send_pages,
        tables,
        lengths,
        kcache,
        vcache,
        queries,
        new_keys,
        new_values,
        pre_mix,
        post_mix,
    )


def solution(mesh):
    in_specs = (
        P(("parts", "dp"), None, "tp"),
        P(("parts", "dp"), None, "tp"),
        P(("parts", "dp"), None, None),
        P(("parts", "dp"), None),
        P(("parts", "dp")),
        P(("parts", "dp"), None, "tp"),
        P(("parts", "dp"), None, "tp"),
        P(("parts", "dp"), None, "tp"),
        P(),
        P(),
    )
    out_specs = P(("parts", "dp"), None, "tp")
    return jax.shard_map(
        functools.partial(on_device, mesh.shape["dp"], mesh.shape["tp"]),
        mesh=mesh,
        in_specs=in_specs,
        out_specs=out_specs,
        check_vma=False,
    )
```

```python
import functools

import jax
import jax.numpy as jnp
from jax import lax
from jax.experimental import pallas as pl
from jax.experimental.pallas import tpu as pltpu
from jax.sharding import PartitionSpec as P

HEAD = 128
MESH = pl.DeviceIdType.MESH
HIGHEST = lax.Precision.HIGHEST


def each(count, body):
    if count <= 4:
        for step in range(count):
            body(step)
    else:

        def looped(step, carry):
            body(step)
            return carry

        lax.fori_loop(0, count, looped, 0)


def kernel(
    n_dp,
    n_tp,
    send_hbm,
    tables_hbm,
    lengths_hbm,
    kcache_ref,
    vcache_ref,
    queries_hbm,
    newk_hbm,
    newv_hbm,
    pre_hbm,
    post_hbm,
    out_ref,
    send_ref,
    tables_ref,
    lengths_ref,
    queries_ref,
    newk_ref,
    newv_ref,
    pre_ref,
    post_ref,
    ext_k,
    ext_v,
    stage_k,
    stage_v,
    in_k,
    in_v,
    q_rows,
    key_rows,
    value_rows,
    raw_send,
    raw_all,
    mix_t,
    blend_send,
    blend_in,
    res,
    load_sem,
    small_sem,
    ks_sem,
    kr_sem,
    vs_sem,
    vr_sem,
    rs_sem,
    rr_sem,
    bs_sem,
    br_sem,
):
    pages, page_len, width = kcache_ref.shape
    cap = send_ref.shape[0]
    slots, maxp = tables_ref.shape
    steps = queries_ref.shape[1]
    heads = queries_ref.shape[2] // HEAD
    groups = width // HEAD
    group_size = heads // groups
    span = maxp * page_len
    dp = lax.axis_index("dp")
    tp = lax.axis_index("tp")

    barrier = pltpu.get_barrier_semaphore()
    for o in range(1, n_dp):
        pl.semaphore_signal(
            barrier, inc=1, device_id={"dp": lax.rem(dp + o, n_dp)}, device_id_type=MESH
        )
    for o in range(1, n_tp):
        pl.semaphore_signal(
            barrier, inc=1, device_id={"tp": lax.rem(tp + o, n_tp)}, device_id_type=MESH
        )

    parts = load_sem.shape[1]
    chunk = pages // parts

    def load(which, cache, ext, part):
        rows = pl.ds(part * chunk, chunk)
        return pltpu.make_async_copy(cache.at[rows], ext.at[rows], load_sem.at[which, part])

    small = [
        pltpu.make_async_copy(source, target, small_sem.at[i])
        for i, (source, target) in enumerate(
            (
                (send_hbm, send_ref),
                (tables_hbm, tables_ref),
                (lengths_hbm, lengths_ref),
                (queries_hbm, queries_ref),
                (newk_hbm, newk_ref),
                (newv_hbm, newv_ref),
                (pre_hbm, pre_ref),
                (post_hbm, post_ref),
            )
        )
    ]
    small[0].start()
    for part in range(parts):
        load(0, kcache_ref, ext_k, part).start()
    for copy in small[1:]:
        copy.start()
    for part in range(parts):
        load(1, vcache_ref, ext_v, part).start()

    def target_of(o):
        return lax.rem(dp + o + 1, n_dp)

    def key_copy(g, o):
        return pltpu.make_async_remote_copy(
            src_ref=stage_k.at[g, pl.ds(o * cap, cap)],
            dst_ref=in_k.at[g, pl.ds(dp * cap, cap)],
            send_sem=ks_sem.at[g, o],
            recv_sem=kr_sem.at[g, o],
            device_id={"dp": target_of(o)},
            device_id_type=MESH,
        )

    def value_copy(o):
        return pltpu.make_async_remote_copy(
            src_ref=stage_v.at[pl.ds(o * cap, cap)],
            dst_ref=in_v.at[pl.ds(dp * cap, cap)],
            send_sem=vs_sem.at[o],
            recv_sem=vr_sem.at[o],
            device_id={"dp": target_of(o)},
            device_id_type=MESH,
        )

    def listed(o, c):
        return jnp.maximum(send_ref[c, 0, target_of(o)], 0)

    def columns(g):
        return slice(g * HEAD, (g + 1) * HEAD)

    small[0].wait()
    pl.semaphore_wait(barrier, n_dp + n_tp - 2)
    for part in range(parts):
        load(0, kcache_ref, ext_k, part).wait()

    for g in range(groups):

        def send_k(o):
            for c in range(cap):
                stage_k[g, o * cap + c] = ext_k[listed(o, c), :, columns(g)]
            key_copy(g, o).start()

        each(n_dp - 1, send_k)

    for copy in small[1:]:
        copy.wait()

    for s in range(slots):
        for h in range(heads):
            g, r = h // group_size, h % group_size
            q_rows[s, g, pl.ds(r, steps, stride=group_size), :] = queries_ref[
                s, :, columns(h)
            ].astype(jnp.float32)
    mix_t[0] = pre_ref[...].T
    mix_t[1] = post_ref[...].T

    for part in range(parts):
        load(1, vcache_ref, ext_v, part).wait()

    def stage_values(o):
        for c in range(cap):
            stage_v[o * cap + c] = ext_v[listed(o, c)]

    each(n_dp - 1, stage_values)

    position = lax.broadcasted_iota(jnp.int32, (steps * group_size, span), 1)

    def raw_of(g, s):
        for p in range(maxp):
            key_rows[pl.ds(p * page_len, page_len), :] = ext_k[
                tables_ref[s, p], :, columns(g)
            ]
        rows = q_rows[s, g].astype(jnp.bfloat16)
        contract = (((1,), (1,)), ((), ()))
        raw = lax.dot_general(
            rows, key_rows[...], contract, preferred_element_type=jnp.float32
        )
        fresh = lax.dot_general(
            rows, newk_ref[s, :, columns(g)], contract, preferred_element_type=jnp.float32
        )
        first = lengths_ref[s]
        for t in range(steps):
            raw = jnp.where(position == first + t, fresh[:, t : t + 1], raw)
        return (raw * (HEAD ** (-0.5))).reshape(steps, group_size, span)

    def raw_copy(g, o, first, count):
        which = pl.ds(first, count)
        return pltpu.make_async_remote_copy(
            src_ref=raw_send.at[o - 1, g, which],
            dst_ref=raw_all.at[which, pl.ds(tp * heads + g * group_size, group_size)],
            send_sem=rs_sem.at[o - 1, g, first],
            recv_sem=rr_sem.at[o - 1, g, first],
            device_id={"tp": lax.rem(tp + o, n_tp)},
            device_id_type=MESH,
        )

    half = n_tp // 2
    order = [half] + [o for o in range(1, n_tp) if o != half]
    last = groups - 1
    for g in range(groups):

        def take_in(o):
            key_copy(g, o).wait_recv()
            source = lax.rem(dp + n_dp - 1 - o, n_dp)
            for c in range(cap):
                ext_k[pages + source * cap + c, :, columns(g)] = in_k[g, source * cap + c]

        each(n_dp - 1, take_in)
        if g == last:
            each(n_dp - 1, lambda o: value_copy(o).start())
        for o in order:
            raw_send[o - 1, g] = raw_of(g, lax.rem(tp + o, n_tp))
            if g < last:
                raw_copy(g, o, 0, steps).start()
            else:
                raw_copy(g, o, 0, 1).start()
        if g == last:
            for t in range(1, steps):
                for o in order:
                    raw_copy(g, o, t, 1).start()
        raw_all[:, pl.ds(tp * heads + g * group_size, group_size), :] = raw_of(g, tp)

    def blend_copy(o, t):
        peer = lax.rem(tp + o, n_tp)
        return pltpu.make_async_remote_copy(
            src_ref=blend_send.at[t, pl.ds(peer * heads, heads)],
            dst_ref=blend_in.at[tp, pl.ds(t * heads, heads)],
            send_sem=bs_sem.at[o - 1, t],
            recv_sem=br_sem.at[o - 1, t],
            device_id={"tp": peer},
            device_id_type=MESH,
        )

    spot = lax.broadcasted_iota(jnp.int32, (n_tp * heads, span), 1)
    own_length = lengths_ref[tp]

    def mix(t):
        for o in order:
            if t == 0:
                for g in range(last):
                    raw_copy(g, o, 0, steps).wait_recv()
            raw_copy(last, o, t, 1).wait_recv()
        mixed = jnp.dot(
            mix_t[0], raw_all[t], precision=HIGHEST, preferred_element_type=jnp.float32
        )
        mixed = jnp.where(spot <= own_length + t, mixed, -jnp.inf)
        raised = jnp.exp(mixed - jnp.max(mixed, axis=1, keepdims=True))
        weights = raised / jnp.sum(raised, axis=1, keepdims=True)
        blended = jnp.dot(
            mix_t[1], weights, precision=HIGHEST, preferred_element_type=jnp.float32
        )
        blend_send[t] = blended.astype(jnp.bfloat16)
        for o in order:
            blend_copy(o, t).start()
        blend_in[tp, pl.ds(t * heads, heads), :] = blend_send[t, pl.ds(tp * heads, heads), :]

    row = lax.broadcasted_iota(jnp.int32, (page_len, width), 0)

    def gather_values(s):
        first = lengths_ref[s]
        fresh = newv_ref[s].astype(jnp.float32)
        for p in range(maxp):
            page = ext_v[tables_ref[s, p]].astype(jnp.float32)
            for t in range(steps):
                page = jnp.where(row == first + t - p * page_len, fresh[t : t + 1, :], page)
            value_rows[s, pl.ds(p * page_len, page_len), :] = page.astype(jnp.bfloat16)

    for t in range(steps - 1):
        mix(t)

    def take_in_values(o):
        value_copy(o).wait_recv()
        source = lax.rem(dp + n_dp - 1 - o, n_dp)
        for c in range(cap):
            ext_v[pages + source * cap + c] = in_v[source * cap + c]

    each(n_dp - 1, take_in_values)
    for s in range(slots):
        gather_values(s)
    mix(steps - 1)

    for o in [0] + [n_tp - o for o in order]:
        s = lax.rem(tp + o, n_tp)
        if o:
            for t in range(steps):
                blend_copy(n_tp - o, t).wait_recv()
        result = jnp.dot(blend_in[s], value_rows[s], preferred_element_type=jnp.float32)
        for g in range(groups):
            res[g] = result[:, g * HEAD : (g + 1) * HEAD]
        for h in range(heads):
            out_ref[s, :, h * HEAD : (h + 1) * HEAD] = res[
                h // group_size, pl.ds(h, steps, stride=heads), :
            ].astype(out_ref.dtype)

    def all_sent(o):
        for g in range(groups):
            key_copy(g, o).wait_send()
        value_copy(o).wait_send()

    each(n_dp - 1, all_sent)
    for o in order:
        for g in range(last):
            raw_copy(g, o, 0, steps).wait_send()
        for t in range(steps):
            raw_copy(last, o, t, 1).wait_send()
            blend_copy(o, t).wait_send()


def on_device(
    n_dp,
    n_tp,
    kcache,
    vcache,
    send_pages,
    tables,
    lengths,
    queries,
    new_keys,
    new_values,
    pre_mix,
    post_mix,
):
    pages, page_len, width = kcache.shape
    send_pages = jnp.transpose(send_pages, (2, 0, 1))
    cap = send_pages.shape[0]
    slots, maxp = tables.shape
    steps = queries.shape[1]
    heads = queries.shape[2] // HEAD
    groups = width // HEAD
    span = maxp * page_len
    all_heads = heads * n_tp
    load_parts = 4
    vmem = pl.BlockSpec(memory_space=pltpu.VMEM)
    hbm = pl.BlockSpec(memory_space=pltpu.HBM)
    moved = (n_dp - 1) * cap
    bf16, f32 = jnp.bfloat16, jnp.float32
    dma = pltpu.SemaphoreType.DMA
    return pl.pallas_call(
        functools.partial(kernel, n_dp, n_tp),
        out_shape=jax.ShapeDtypeStruct(queries.shape, bf16),
        in_specs=[hbm] * 10,
        out_specs=vmem,
        scratch_shapes=[
            pltpu.SMEM(send_pages.shape, jnp.int32),
            pltpu.SMEM(tables.shape, jnp.int32),
            pltpu.SMEM(lengths.shape, jnp.int32),
            pltpu.VMEM(queries.shape, bf16),
            pltpu.VMEM(new_keys.shape, bf16),
            pltpu.VMEM(new_values.shape, bf16),
            pltpu.VMEM(pre_mix.shape, f32),
            pltpu.VMEM(post_mix.shape, f32),
            pltpu.VMEM((pages + n_dp * cap, page_len, width), bf16),
            pltpu.VMEM((pages + n_dp * cap, page_len, width), bf16),
            pltpu.VMEM((groups, moved, page_len, HEAD), bf16),
            pltpu.VMEM((moved, page_len, width), bf16),
            pltpu.VMEM((groups, n_dp * cap, page_len, HEAD), bf16),
            pltpu.VMEM((n_dp * cap, page_len, width), bf16),
            pltpu.VMEM((slots, groups, steps * heads // groups, HEAD), f32),
            pltpu.VMEM((span, HEAD), bf16),
            pltpu.VMEM((slots, span, width), bf16),
            pltpu.VMEM((n_tp - 1, groups, steps, heads // groups, span), f32),
            pltpu.VMEM((steps, all_heads, span), f32),
            pltpu.VMEM((2, all_heads, all_heads), f32),
            pltpu.VMEM((steps, all_heads, span), bf16),
            pltpu.VMEM((slots, steps * heads, span), bf16),
            pltpu.VMEM((groups, steps * heads, HEAD), f32),
            dma((2, load_parts)),
            dma((8,)),
            dma((groups, n_dp - 1)),
            dma((groups, n_dp - 1)),
            dma((n_dp - 1,)),
            dma((n_dp - 1,)),
            dma((n_tp - 1, groups, steps)),
            dma((n_tp - 1, groups, steps)),
            dma((n_tp - 1, steps)),
            dma((n_tp - 1, steps)),
        ],
        compiler_params=pltpu.CompilerParams(
            collective_id=0, has_side_effects=True, vmem_limit_bytes=64 * 1024 * 1024
        ),
    )(
        send_pages,
        tables,
        lengths,
        kcache,
        vcache,
        queries,
        new_keys,
        new_values,
        pre_mix,
        post_mix,
    )


def solution(mesh):
    in_specs = (
        P(("parts", "dp"), None, "tp"),
        P(("parts", "dp"), None, "tp"),
        P(("parts", "dp"), None, None),
        P(("parts", "dp"), None),
        P(("parts", "dp")),
        P(("parts", "dp"), None, "tp"),
        P(("parts", "dp"), None, "tp"),
        P(("parts", "dp"), None, "tp"),
        P(),
        P(),
    )
    out_specs = P(("parts", "dp"), None, "tp")
    return jax.shard_map(
        functools.partial(on_device, mesh.shape["dp"], mesh.shape["tp"]),
        mesh=mesh,
        in_specs=in_specs,
        out_specs=out_specs,
        check_vma=False,
    )
```

```python
import functools

import jax
import jax.numpy as jnp
from jax import lax
from jax.experimental import pallas as pl
from jax.experimental.pallas import tpu as pltpu
from jax.sharding import PartitionSpec as P

HEAD = 128
MESH = pl.DeviceIdType.MESH
HIGHEST = lax.Precision.HIGHEST


def each(count, body):
    if count <= 4:
        for step in range(count):
            body(step)
    else:

        def looped(step, carry):
            body(step)
            return carry

        lax.fori_loop(0, count, looped, 0)


def kernel(
    n_dp,
    n_tp,
    send_hbm,
    tables_hbm,
    lengths_hbm,
    kcache_ref,
    vcache_ref,
    queries_hbm,
    newk_hbm,
    newv_hbm,
    pre_hbm,
    post_hbm,
    out_ref,
    send_ref,
    tables_ref,
    lengths_ref,
    queries_ref,
    newk_ref,
    newv_ref,
    pre_ref,
    post_ref,
    ext_k,
    ext_v,
    stage_k,
    stage_v,
    in_k,
    in_v,
    q_rows,
    key_rows,
    value_rows,
    raw_send,
    raw_all,
    mix_t,
    blend_send,
    blend_in,
    res,
    load_sem,
    small_sem,
    ks_sem,
    kr_sem,
    vs_sem,
    vr_sem,
    rs_sem,
    rr_sem,
    bs_sem,
    br_sem,
):
    pages, page_len, width = kcache_ref.shape
    cap = send_ref.shape[0]
    slots, maxp = tables_ref.shape
    steps = queries_ref.shape[1]
    heads = queries_ref.shape[2] // HEAD
    groups = width // HEAD
    group_size = heads // groups
    span = maxp * page_len
    dp = lax.axis_index("dp")
    tp = lax.axis_index("tp")

    barrier = pltpu.get_barrier_semaphore()
    for o in range(1, n_dp):
        pl.semaphore_signal(
            barrier, inc=1, device_id={"dp": lax.rem(dp + o, n_dp)}, device_id_type=MESH
        )
    for o in range(1, n_tp):
        pl.semaphore_signal(
            barrier, inc=1, device_id={"tp": lax.rem(tp + o, n_tp)}, device_id_type=MESH
        )

    parts = load_sem.shape[1]
    chunk = pages // parts

    def load(which, cache, ext, part):
        rows = pl.ds(part * chunk, chunk)
        return pltpu.make_async_copy(cache.at[rows], ext.at[rows], load_sem.at[which, part])

    small = [
        pltpu.make_async_copy(source, target, small_sem.at[i])
        for i, (source, target) in enumerate(
            (
                (send_hbm, send_ref),
                (tables_hbm, tables_ref),
                (lengths_hbm, lengths_ref),
                (queries_hbm, queries_ref),
                (newk_hbm, newk_ref),
                (newv_hbm, newv_ref),
                (pre_hbm, pre_ref),
                (post_hbm, post_ref),
            )
        )
    ]
    small[0].start()
    for part in range(parts):
        load(0, kcache_ref, ext_k, part).start()
    for copy in small[1:]:
        copy.start()
    for part in range(parts):
        load(1, vcache_ref, ext_v, part).start()

    def target_of(o):
        return lax.rem(dp + o + 1, n_dp)

    def key_copy(g, o):
        return pltpu.make_async_remote_copy(
            src_ref=stage_k.at[g, pl.ds(o * cap, cap)],
            dst_ref=in_k.at[g, pl.ds(dp * cap, cap)],
            send_sem=ks_sem.at[g, o],
            recv_sem=kr_sem.at[g, o],
            device_id={"dp": target_of(o)},
            device_id_type=MESH,
        )

    def value_copy(o):
        return pltpu.make_async_remote_copy(
            src_ref=stage_v.at[pl.ds(o * cap, cap)],
            dst_ref=in_v.at[pl.ds(dp * cap, cap)],
            send_sem=vs_sem.at[o],
            recv_sem=vr_sem.at[o],
            device_id={"dp": target_of(o)},
            device_id_type=MESH,
        )

    def listed(o, c):
        return jnp.maximum(send_ref[c, 0, target_of(o)], 0)

    def columns(g):
        return slice(g * HEAD, (g + 1) * HEAD)

    small[0].wait()
    pl.semaphore_wait(barrier, n_dp + n_tp - 2)
    for part in range(parts):
        load(0, kcache_ref, ext_k, part).wait()

    for g in range(groups):

        def send_k(o):
            for c in range(cap):
                stage_k[g, o * cap + c] = ext_k[listed(o, c), :, columns(g)]
            key_copy(g, o).start()

        each(n_dp - 1, send_k)

    for copy in small[1:]:
        copy.wait()

    for s in range(slots):
        for h in range(heads):
            g, r = h // group_size, h % group_size
            q_rows[s, g, pl.ds(r, steps, stride=group_size), :] = queries_ref[
                s, :, columns(h)
            ].astype(jnp.float32)
    mix_t[0] = pre_ref[...].T
    mix_t[1] = post_ref[...].T

    for part in range(parts):
        load(1, vcache_ref, ext_v, part).wait()

    def stage_values(o):
        for c in range(cap):
            stage_v[o * cap + c] = ext_v[listed(o, c)]

    each(n_dp - 1, stage_values)

    position = lax.broadcasted_iota(jnp.int32, (steps * group_size, span), 1)

    def raw_of(g, s):
        for p in range(maxp):
            key_rows[pl.ds(p * page_len, page_len), :] = ext_k[
                tables_ref[s, p], :, columns(g)
            ]
        rows = q_rows[s, g].astype(jnp.bfloat16)
        contract = (((1,), (1,)), ((), ()))
        raw = lax.dot_general(
            rows, key_rows[...], contract, preferred_element_type=jnp.float32
        )
        fresh = lax.dot_general(
            rows, newk_ref[s, :, columns(g)], contract, preferred_element_type=jnp.float32
        )
        first = lengths_ref[s]
        for t in range(steps):
            raw = jnp.where(position == first + t, fresh[:, t : t + 1], raw)
        return (raw * (HEAD ** (-0.5))).reshape(steps, group_size, span)

    def raw_copy(g, o, first, count):
        which = pl.ds(first, count)
        return pltpu.make_async_remote_copy(
            src_ref=raw_send.at[o - 1, g, which],
            dst_ref=raw_all.at[which, pl.ds(tp * heads + g * group_size, group_size)],
            send_sem=rs_sem.at[o - 1, g, first],
            recv_sem=rr_sem.at[o - 1, g, first],
            device_id={"tp": lax.rem(tp + o, n_tp)},
            device_id_type=MESH,
        )

    half = n_tp // 2
    order = [half] + [o for o in range(1, n_tp) if o != half]
    last = groups - 1
    for g in range(groups):

        def take_in(o):
            key_copy(g, o).wait_recv()
            source = lax.rem(dp + n_dp - 1 - o, n_dp)
            for c in range(cap):
                ext_k[pages + source * cap + c, :, columns(g)] = in_k[g, source * cap + c]

        each(n_dp - 1, take_in)
        if g == last:
            each(n_dp - 1, lambda o: value_copy(o).start())
        for o in order:
            raw_send[o - 1, g] = raw_of(g, lax.rem(tp + o, n_tp))
            if g < last:
                raw_copy(g, o, 0, steps).start()
            else:
                raw_copy(g, o, 0, 1).start()
        if g == last:
            for t in range(1, steps):
                for o in order:
                    raw_copy(g, o, t, 1).start()
        raw_all[:, pl.ds(tp * heads + g * group_size, group_size), :] = raw_of(g, tp)

    def blend_copy(o, t):
        peer = lax.rem(tp + o, n_tp)
        return pltpu.make_async_remote_copy(
            src_ref=blend_send.at[t, pl.ds(peer * heads, heads)],
            dst_ref=blend_in.at[tp, pl.ds(t * heads, heads)],
            send_sem=bs_sem.at[o - 1, t],
            recv_sem=br_sem.at[o - 1, t],
            device_id={"tp": peer},
            device_id_type=MESH,
        )

    spot = lax.broadcasted_iota(jnp.int32, (n_tp * heads, span), 1)
    own_length = lengths_ref[tp]

    def mix(t):
        for o in order:
            if t == 0:
                for g in range(last):
                    raw_copy(g, o, 0, steps).wait_recv()
            raw_copy(last, o, t, 1).wait_recv()
        mixed = jnp.dot(
            mix_t[0], raw_all[t], precision=HIGHEST, preferred_element_type=jnp.float32
        )
        mixed = jnp.where(spot <= own_length + t, mixed, -jnp.inf)
        raised = jnp.exp(mixed - jnp.max(mixed, axis=1, keepdims=True))
        weights = raised / jnp.sum(raised, axis=1, keepdims=True)
        blended = jnp.dot(
            mix_t[1], weights, precision=HIGHEST, preferred_element_type=jnp.float32
        )
        blend_send[t] = blended.astype(jnp.bfloat16)
        for o in order:
            blend_copy(o, t).start()
        blend_in[tp, pl.ds(t * heads, heads), :] = blend_send[t, pl.ds(tp * heads, heads), :]

    row = lax.broadcasted_iota(jnp.int32, (page_len, width), 0)

    def gather_values(s):
        first = lengths_ref[s]
        fresh = newv_ref[s].astype(jnp.float32)
        for p in range(maxp):
            page = ext_v[tables_ref[s, p]].astype(jnp.float32)
            for t in range(steps):
                page = jnp.where(row == first + t - p * page_len, fresh[t : t + 1, :], page)
            value_rows[s, pl.ds(p * page_len, page_len), :] = page.astype(jnp.bfloat16)


    def take_in_values(o):
        value_copy(o).wait_recv()
        source = lax.rem(dp + n_dp - 1 - o, n_dp)
        for c in range(cap):
            ext_v[pages + source * cap + c] = in_v[source * cap + c]

    each(n_dp - 1, take_in_values)
    for s in range(slots):
        gather_values(s)
    for t in range(steps):
        mix(t)

    for o in [0] + [n_tp - o for o in order]:
        s = lax.rem(tp + o, n_tp)
        if o:
            for t in range(steps):
                blend_copy(n_tp - o, t).wait_recv()
        result = jnp.dot(blend_in[s], value_rows[s], preferred_element_type=jnp.float32)
        for g in range(groups):
            res[g] = result[:, g * HEAD : (g + 1) * HEAD]
        for h in range(heads):
            out_ref[s, :, h * HEAD : (h + 1) * HEAD] = res[
                h // group_size, pl.ds(h, steps, stride=heads), :
            ].astype(out_ref.dtype)

    def all_sent(o):
        for g in range(groups):
            key_copy(g, o).wait_send()
        value_copy(o).wait_send()

    each(n_dp - 1, all_sent)
    for o in order:
        for g in range(last):
            raw_copy(g, o, 0, steps).wait_send()
        for t in range(steps):
            raw_copy(last, o, t, 1).wait_send()
            blend_copy(o, t).wait_send()


def on_device(
    n_dp,
    n_tp,
    kcache,
    vcache,
    send_pages,
    tables,
    lengths,
    queries,
    new_keys,
    new_values,
    pre_mix,
    post_mix,
):
    pages, page_len, width = kcache.shape
    send_pages = jnp.transpose(send_pages, (2, 0, 1))
    cap = send_pages.shape[0]
    slots, maxp = tables.shape
    steps = queries.shape[1]
    heads = queries.shape[2] // HEAD
    groups = width // HEAD
    span = maxp * page_len
    all_heads = heads * n_tp
    load_parts = 4
    vmem = pl.BlockSpec(memory_space=pltpu.VMEM)
    hbm = pl.BlockSpec(memory_space=pltpu.HBM)
    moved = (n_dp - 1) * cap
    bf16, f32 = jnp.bfloat16, jnp.float32
    dma = pltpu.SemaphoreType.DMA
    return pl.pallas_call(
        functools.partial(kernel, n_dp, n_tp),
        out_shape=jax.ShapeDtypeStruct(queries.shape, bf16),
        in_specs=[hbm] * 10,
        out_specs=vmem,
        scratch_shapes=[
            pltpu.SMEM(send_pages.shape, jnp.int32),
            pltpu.SMEM(tables.shape, jnp.int32),
            pltpu.SMEM(lengths.shape, jnp.int32),
            pltpu.VMEM(queries.shape, bf16),
            pltpu.VMEM(new_keys.shape, bf16),
            pltpu.VMEM(new_values.shape, bf16),
            pltpu.VMEM(pre_mix.shape, f32),
            pltpu.VMEM(post_mix.shape, f32),
            pltpu.VMEM((pages + n_dp * cap, page_len, width), bf16),
            pltpu.VMEM((pages + n_dp * cap, page_len, width), bf16),
            pltpu.VMEM((groups, moved, page_len, HEAD), bf16),
            pltpu.VMEM((moved, page_len, width), bf16),
            pltpu.VMEM((groups, n_dp * cap, page_len, HEAD), bf16),
            pltpu.VMEM((n_dp * cap, page_len, width), bf16),
            pltpu.VMEM((slots, groups, steps * heads // groups, HEAD), f32),
            pltpu.VMEM((span, HEAD), bf16),
            pltpu.VMEM((slots, span, width), bf16),
            pltpu.VMEM((n_tp - 1, groups, steps, heads // groups, span), f32),
            pltpu.VMEM((steps, all_heads, span), f32),
            pltpu.VMEM((2, all_heads, all_heads), f32),
            pltpu.VMEM((steps, all_heads, span), bf16),
            pltpu.VMEM((slots, steps * heads, span), bf16),
            pltpu.VMEM((groups, steps * heads, HEAD), f32),
            dma((2, load_parts)),
            dma((8,)),
            dma((groups, n_dp - 1)),
            dma((groups, n_dp - 1)),
            dma((n_dp - 1,)),
            dma((n_dp - 1,)),
            dma((n_tp - 1, groups, steps)),
            dma((n_tp - 1, groups, steps)),
            dma((n_tp - 1, steps)),
            dma((n_tp - 1, steps)),
        ],
        compiler_params=pltpu.CompilerParams(
            collective_id=0, has_side_effects=True, vmem_limit_bytes=64 * 1024 * 1024
        ),
    )(
        send_pages,
        tables,
        lengths,
        kcache,
        vcache,
        queries,
        new_keys,
        new_values,
        pre_mix,
        post_mix,
    )


def solution(mesh):
    in_specs = (
        P(("parts", "dp"), None, "tp"),
        P(("parts", "dp"), None, "tp"),
        P(("parts", "dp"), None, None),
        P(("parts", "dp"), None),
        P(("parts", "dp")),
        P(("parts", "dp"), None, "tp"),
        P(("parts", "dp"), None, "tp"),
        P(("parts", "dp"), None, "tp"),
        P(),
        P(),
    )
    out_specs = P(("parts", "dp"), None, "tp")
    return jax.shard_map(
        functools.partial(on_device, mesh.shape["dp"], mesh.shape["tp"]),
        mesh=mesh,
        in_specs=in_specs,
        out_specs=out_specs,
        check_vma=False,
    )
```
